32 devices in a mesh: pipe: 8 (over y, x, core), dp: 4 (over z).
Axes of the slice: x: 2, y: 2, z: 4, core: 2. Of those that a mesh axis runs over, the one named last changes fastest.
Arguments:
- inputs: bfloat16 [4, 384, 3072], P(None, 'dp'), may hold values from -24 to 24
- projection: bfloat16 [8, 3072, 3072], P('pipe'), may hold values from -0.109375 to 0.109375
- cotangent: bfloat16 [4, 384, 3072], P(None, 'dp'), may hold values from -6 to 6
Outputs:
- weight_grad: bfloat16 [8, 3072, 3072], P('pipe', 'dp')
The draws below stay inside these ranges and needn't reach their ends.
All inputs are finite; a program needn't handle non-finite values.
Results may differ from the reference program's by a relative error of at most 0.033.
Values may be sent and summed in bfloat16 or wider, within the bound.
A program may use at most 192 MiB of HBM per device.

```python
import math
import jax
import jax.numpy as jnp
from jax import lax

D = 3072
MICRO = 4
TOK_MB = 96
SECTIONS = 8
TOKENS = 384
N_DP = 4


def draw_inputs(key, part):
    key_base, key_rows, key_cols = jax.random.split(key, 3)
    base_values = jnp.clip(jax.random.normal(key_base, (MICRO, TOKENS, D), jnp.float32), -6.0, 6.0)
    low_scale = 0.3
    high_scale = 3.0
    row_scales = jnp.exp(jax.random.uniform(key_rows, (MICRO, TOKENS, 1), jnp.float32, math.log(low_scale), math.log(high_scale)))
    column_scales = jnp.exp(jax.random.uniform(key_cols, (1, 1, D), jnp.float32, math.log(low_scale), math.log(high_scale)))
    return jnp.clip(base_values * row_scales * column_scales, -24.0, 24.0).astype(jnp.bfloat16)


def levels(own_key, extent, pieces, smallest, top_value):
    loudness, own = 1.0, jax.random.fold_in(own_key, 6)
    for dim, shards_of in pieces:
        heights = jnp.exp(jax.random.uniform(jax.random.fold_in(own, dim), (shards_of,), jnp.float32, smallest / len(pieces), top_value / len(pieces)))
        loudness = loudness * jnp.repeat(heights, extent[dim] // shards_of).reshape([-1 if axis == dim else 1 for axis in range(len(extent))])
    return loudness


def centred(stream_key, extent, spread, limit, cuts=(), held_as=jnp.bfloat16):
    array = jax.random.normal(stream_key, extent, jnp.float32) * spread
    if len(cuts) > 0:
        array = levels(stream_key, extent, cuts, -0.22, 0.18) * array
    return jnp.clip(array, min=-limit, max=limit).astype(held_as)


def setup_inputs(seed: int = 0) -> dict:
    key_list = jax.random.split(jax.random.key(seed), 4)
    return {
        "inputs": draw_inputs(jax.random.fold_in(key_list[3], 71), 0),
        "projection": centred(key_list[1], (SECTIONS, D, D), D ** -0.5, 0.109375, ((0, 8),)),
        "cotangent": centred(key_list[2], (MICRO, TOKENS, D), 1.0, 6.0, ((1, 4),)),
    }


EPSILON = 1e-06

def norm_factor(values):
    floats = values.astype(jnp.float32)
    factor = lax.rsqrt(lax.optimization_barrier(jnp.mean(floats * floats, axis=-1, keepdims=True)) + EPSILON)
    return (floats, factor)

def forward_layer(values, weight):
    floats, factor = norm_factor(values)
    normed = (floats * factor).astype(jnp.bfloat16)
    gate_value = jnp.dot(normed, weight, preferred_element_type=jnp.float32)
    output = (floats + jax.nn.silu(gate_value)).astype(jnp.bfloat16)
    return (output, gate_value)

def backward_layer(values, gate_value, upstream, weight):
    floats, factor = norm_factor(values)
    up_float = upstream.astype(jnp.float32)
    sigma = jax.nn.sigmoid(gate_value)
    slope = (up_float * sigma * (1.0 + gate_value * (1.0 - sigma))).astype(jnp.bfloat16)
    back = jnp.dot(slope, weight.T, preferred_element_type=jnp.float32)
    unit = floats * factor
    down = (up_float + factor * (back - unit * lax.optimization_barrier(jnp.mean(back * unit, axis=-1, keepdims=True)))).astype(jnp.bfloat16)
    normed = (floats * factor).astype(jnp.bfloat16)
    return (down, slope, normed)

def replica_sum(normed, slope):
    left_rows = normed.reshape(MICRO, N_DP, TOK_MB, D).transpose(1, 0, 2, 3).reshape(N_DP, MICRO * TOK_MB, D)
    right_rows = slope.reshape(MICRO, N_DP, TOK_MB, D).transpose(1, 0, 2, 3).reshape(N_DP, MICRO * TOK_MB, D)

    def add_replica(total, pair):
        left_part, right_part = pair
        partial_term = jnp.dot(left_part.T, right_part, preferred_element_type=jnp.float32)
        rounded = lax.optimization_barrier(partial_term.astype(jnp.bfloat16))
        return (total + rounded.astype(jnp.float32), None)
    total, unused = lax.scan(add_replica, jnp.zeros((D, D), jnp.float32), (left_rows, right_rows))
    factor = 1.0 / math.sqrt(MICRO * TOKENS)
    return (total * factor).astype(jnp.bfloat16)

def reference(inputs, projection, cotangent):
    flat_inputs = inputs.reshape(MICRO * TOKENS, D)
    kept_inputs = []
    kept_gates = []
    current = flat_inputs
    for section in range(SECTIONS):
        kept_inputs.append(current)
        current, gate_value = forward_layer(current, projection[section])
        kept_gates.append(gate_value)
    upstream = cotangent.reshape(MICRO * TOKENS, D)
    grads = [None] * SECTIONS
    for section in reversed(range(SECTIONS)):
        down, slope, normed = backward_layer(kept_inputs[section], kept_gates[section], upstream, projection[section])
        grads[section] = replica_sum(normed.reshape(MICRO, TOKENS, D), slope.reshape(MICRO, TOKENS, D))
        upstream = down
    return jnp.stack(grads)
```

```python
import functools
import math

import jax
import jax.numpy as jnp
from jax import lax
from jax.experimental import pallas as pl
from jax.experimental.pallas import tpu as pltpu
from jax.sharding import PartitionSpec as P

EPSILON = 1e-06
TILE = 512
OUT_TILE = 256


def relay_kernel(
    micro, sections, replicas,
    in_ref, w_hbm, cot_ref, out_ref,
    w, xs, acts, gates, ups, slopes, normed, normed_in, normed_t, facs,
    w_sem, first_sem, cot_sem, act_send, act_recv, down_send, down_recv,
    norm_send, norm_recv, right_send, left_send, slope_recv,
):
    section = lax.axis_index("pipe")
    me = lax.axis_index("dp")
    tokens, width = xs.shape
    rows = tokens // micro
    chunk = width // replicas
    tiles = width // TILE
    is_first = section == 0
    is_last = section == sections - 1
    after = lax.rem(section + 1, sections)
    before = lax.rem(section + sections - 1, sections)

    def rows_of(m):
        return pl.ds(pl.multiple_of(m * rows, rows), rows)

    def cols_of(n):
        return pl.ds(pl.multiple_of(n * TILE, TILE), TILE)

    load_w = pltpu.make_async_copy(w_hbm, w, w_sem)
    load_w.start()

    def load_first(m):
        return pltpu.make_async_copy(in_ref.at[rows_of(m)], xs.at[rows_of(m)], first_sem.at[m])

    def load_cot(m):
        return pltpu.make_async_copy(cot_ref.at[rows_of(m)], ups.at[rows_of(m)], cot_sem.at[m])

    @pl.when(is_first)
    def _():
        @pl.loop(0, micro)
        def _(m):
            load_first(m).start()

    @pl.when(is_last)
    def _():
        @pl.loop(0, micro)
        def _(m):
            load_cot(m).start()

    barrier = pltpu.get_barrier_semaphore()
    for other in (after, before):
        pl.semaphore_signal(barrier, inc=1, device_id={"pipe": other})
    for step in range(1, replicas):
        peer = lax.rem(me + step, replicas)
        pl.semaphore_signal(barrier, inc=1, device_id={"dp": peer})
    pl.semaphore_wait(barrier, 2 + replicas - 1)
    load_w.wait()

    def act_copy(m, cols=None):
        where = (rows_of(m),) if cols is None else (rows_of(m), cols)
        return pltpu.make_async_remote_copy(
            src_ref=acts.at[where], dst_ref=xs.at[where],
            send_sem=act_send.at[m], recv_sem=act_recv.at[m], device_id={"pipe": after},
        )

    def down_copy(m, cols=None):
        where = (rows_of(m),) if cols is None else (rows_of(m), cols)
        return pltpu.make_async_remote_copy(
            src_ref=acts.at[where], dst_ref=ups.at[where],
            send_sem=down_send.at[m], recv_sem=down_recv.at[m], device_id={"pipe": before},
        )

    def norm_copy(m, step):
        peer = lax.rem(me + step, replicas)
        cols = pl.ds(pl.multiple_of(peer * chunk, chunk), chunk)
        return pltpu.make_async_remote_copy(
            src_ref=normed.at[rows_of(m), cols], dst_ref=normed_in.at[me, rows_of(m)],
            send_sem=norm_send.at[step, m], recv_sem=norm_recv.at[step, m],
            device_id={"dp": peer},
        )

    def norm_arrival(m, step):
        origin = lax.rem(me + replicas - step, replicas)
        return pltpu.make_async_remote_copy(
            src_ref=normed.at[rows_of(m), pl.ds(0, chunk)],
            dst_ref=normed_in.at[origin, rows_of(m)],
            send_sem=norm_send.at[step, m], recv_sem=norm_recv.at[step, m],
            device_id={"dp": origin},
        )

    def slope_copy(origin, m, to, sends):
        block = slopes.at[origin, rows_of(m)]
        return pltpu.make_async_remote_copy(
            src_ref=block, dst_ref=block,
            send_sem=sends.at[origin, m], recv_sem=slope_recv.at[origin, m],
            device_id={"dp": to},
        )

    def go_right(origin, m):
        return slope_copy(origin, m, me + 1, right_send)

    def go_left(origin, m):
        return slope_copy(origin, m, me - 1, left_send)

    @pl.loop(0, micro)
    def _(m):
        here = rows_of(m)

        @pl.when(is_first)
        def _():
            load_first(m).wait()

        @pl.when(jnp.logical_not(is_first))
        def _():
            act_copy(m).wait_recv()

        def squares(n, total):
            part = xs[here, cols_of(n)].astype(jnp.float32)
            return total + jnp.sum(part * part, axis=-1, keepdims=True)

        total = lax.fori_loop(0, tiles, squares, jnp.zeros((rows, 1), jnp.float32))
        fac = lax.rsqrt(total / width + EPSILON)
        facs[here, :] = jnp.broadcast_to(fac, (rows, 128))

        @pl.loop(0, tiles)
        def _(n):
            part = xs[here, cols_of(n)].astype(jnp.float32)
            normed[here, cols_of(n)] = (part * fac).astype(jnp.bfloat16)

        for step in range(1, replicas):
            norm_copy(m, step).start()

        @pl.loop(0, tiles)
        def _(n):
            cols = cols_of(n)
            gate = jnp.dot(normed[here, :], w[:, cols], preferred_element_type=jnp.float32)
            gates[here, cols] = gate
            out = xs[here, cols].astype(jnp.float32) + gate / (1.0 + jnp.exp(-gate))
            acts[here, cols] = out.astype(jnp.bfloat16)

            @pl.when(jnp.logical_not(is_last))
            def _():
                act_copy(m, cols).start()

    @pl.when(jnp.logical_not(is_last))
    def _():
        @pl.loop(0, micro)
        def _(m):
            act_copy(m).wait_send()

    @pl.loop(0, micro)
    def _(m):
        here = rows_of(m)

        @pl.when(is_last)
        def _():
            load_cot(m).wait()

        @pl.when(jnp.logical_not(is_last))
        def _():
            down_copy(m).wait_recv()

        @pl.loop(0, tiles)
        def _(n):
            cols = cols_of(n)
            gate = gates[here, cols]
            sig = 1.0 / (1.0 + jnp.exp(-gate))
            up = ups[here, cols].astype(jnp.float32)
            slope = up * sig * (1.0 + gate * (1.0 - sig))
            slopes[me, here, cols] = slope.astype(jnp.bfloat16)

        @pl.when(me < replicas - 1)
        def _():
            go_right(me, m).start()

        @pl.when(me > 0)
        def _():
            go_left(me, m).start()

        fac = facs[here, pl.ds(0, 1)]

        @pl.when(jnp.logical_not(is_first))
        def _():
            def back_tile(n, total):
                cols = cols_of(n)
                back = lax.dot_general(
                    slopes[me, here, :], w[cols, :], (((1,), (1,)), ((), ())),
                    preferred_element_type=jnp.float32,
                )
                gates[here, cols] = back
                unit = xs[here, cols].astype(jnp.float32) * fac
                return total + jnp.sum(back * unit, axis=-1, keepdims=True)

            total = lax.fori_loop(0, tiles, back_tile, jnp.zeros((rows, 1), jnp.float32))
            mean = total / width

            @pl.loop(0, tiles)
            def _(n):
                cols = cols_of(n)
                unit = xs[here, cols].astype(jnp.float32) * fac
                down = ups[here, cols].astype(jnp.float32) + fac * (gates[here, cols] - unit * mean)
                acts[here, cols] = down.astype(jnp.bfloat16)
                down_copy(m, cols).start()

    for step in range(1, replicas):
        @pl.loop(0, micro)
        def _(m):
            norm_arrival(m, step).wait_recv()

    own = pl.ds(pl.multiple_of(me * chunk, chunk), chunk)
    normed_in[me] = normed[:, own]
    for origin in range(replicas):
        normed_t[:, pl.ds(origin * tokens, tokens)] = normed_in[origin].T

    for far in range(1, replicas):
        @pl.loop(0, micro)
        def _(m):
            @pl.when(me - far >= 0)
            def _():
                go_right(me - far, m).wait_recv()

                @pl.when(me < replicas - 1)
                def _():
                    go_right(me - far, m).start()

            @pl.when(me + far < replicas)
            def _():
                go_left(me + far, m).wait_recv()

                @pl.when(me > 0)
                def _():
                    go_left(me + far, m).start()

    scale = 1.0 / math.sqrt(tokens * replicas)

    @pl.loop(0, width // OUT_TILE)
    def _(n):
        cols = pl.ds(pl.multiple_of(n * OUT_TILE, OUT_TILE), OUT_TILE)
        right = slopes[:, :, cols].reshape(replicas * tokens, OUT_TILE)
        total = jnp.dot(normed_t[...], right, preferred_element_type=jnp.float32)
        out_ref[:, cols] = (total * scale).astype(jnp.bfloat16)

    @pl.loop(0, micro)
    def _(m):
        for step in range(1, replicas):
            norm_copy(m, step).wait_send()

        @pl.when(jnp.logical_not(is_first))
        def _():
            down_copy(m).wait_send()

        for origin in range(replicas):
            @pl.when(jnp.logical_and(me >= origin, me < replicas - 1))
            def _():
                go_right(origin, m).wait_send()

            @pl.when(jnp.logical_and(me <= origin, me > 0))
            def _():
                go_left(origin, m).wait_send()


def on_device(sections, replicas, inputs, projection, cotangent):
    micro, rows, width = inputs.shape
    tokens = micro * rows
    chunk = width // replicas
    bf16, f32 = jnp.bfloat16, jnp.float32
    dma = pltpu.SemaphoreType.DMA
    out = pl.pallas_call(
        functools.partial(relay_kernel, micro, sections, replicas),
        out_shape=jax.ShapeDtypeStruct((chunk, width), bf16),
        in_specs=[pl.BlockSpec(memory_space=pl.ANY)] * 3,
        out_specs=pl.BlockSpec(memory_space=pltpu.VMEM),
        scratch_shapes=[
            pltpu.VMEM((width, width), bf16),
            pltpu.VMEM((tokens, width), bf16),
            pltpu.VMEM((tokens, width), bf16),
            pltpu.VMEM((tokens, width), f32),
            pltpu.VMEM((tokens, width), bf16),
            pltpu.VMEM((replicas, tokens, width), bf16),
            pltpu.VMEM((tokens, width), bf16),
            pltpu.VMEM((replicas, tokens, chunk), bf16),
            pltpu.VMEM((chunk, replicas * tokens), bf16),
            pltpu.VMEM((tokens, 128), f32),
            dma, dma((micro,)), dma((micro,)),
            dma((micro,)), dma((micro,)), dma((micro,)), dma((micro,)),
            dma((replicas, micro)), dma((replicas, micro)),
            dma((replicas, micro)), dma((replicas, micro)), dma((replicas, micro)),
        ],
        compiler_params=pltpu.CompilerParams(
            collective_id=0, has_side_effects=True, vmem_limit_bytes=64 * 1024 * 1024
        ),
        cost_estimate=pl.CostEstimate(
            flops=6 * tokens * width * width,
            bytes_accessed=2 * width * (width + 2 * tokens + chunk),
            transcendentals=2 * tokens * width,
        ),
    )(inputs.reshape(tokens, width), projection[0], cotangent.reshape(tokens, width))
    return out[None]


def solution(mesh):
    placed = (P(None, "dp", None), P("pipe", None, None), P(None, "dp", None))
    body = functools.partial(on_device, mesh.shape["pipe"], mesh.shape["dp"])
    return jax.shard_map(
        body, mesh=mesh, in_specs=placed, out_specs=P("pipe", "dp", None), check_vma=False
    )
```

```python
import functools
import math

import jax
import jax.numpy as jnp
from jax import lax
from jax.experimental import pallas as pl
from jax.experimental.pallas import tpu as pltpu
from jax.sharding import PartitionSpec as P

EPSILON = 1e-06
TILE = 512
OUT_TILE = 256


def relay_kernel(
    micro, sections, replicas,
    in_ref, w_hbm, cot_ref, out_ref,
    w, xs, acts, gates, ups, slopes, normed, normed_in, normed_t, facs, sums,
    w_sem, first_sem, cot_sem, act_send, act_recv, down_send, down_recv,
    norm_send, norm_recv, right_send, left_send, slope_recv,
):
    section = lax.axis_index("pipe")
    me = lax.axis_index("dp")
    tokens, width = xs.shape
    rows = tokens // micro
    chunk = width // replicas
    tiles = width // TILE
    is_first = section == 0
    is_last = section == sections - 1
    after = lax.rem(section + 1, sections)
    before = lax.rem(section + sections - 1, sections)

    def rows_of(m):
        return pl.ds(pl.multiple_of(m * rows, rows), rows)

    def cols_of(n):
        return pl.ds(pl.multiple_of(n * TILE, TILE), TILE)

    load_w = pltpu.make_async_copy(w_hbm, w, w_sem)
    load_w.start()

    def load_first(m):
        return pltpu.make_async_copy(in_ref.at[rows_of(m)], xs.at[rows_of(m)], first_sem.at[m])

    def load_cot(m):
        return pltpu.make_async_copy(cot_ref.at[rows_of(m)], ups.at[rows_of(m)], cot_sem.at[m])

    @pl.when(is_first)
    def _():
        @pl.loop(0, micro)
        def _(m):
            load_first(m).start()

    @pl.when(is_last)
    def _():
        @pl.loop(0, micro)
        def _(m):
            load_cot(m).start()

    barrier = pltpu.get_barrier_semaphore()
    for other in (after, before):
        pl.semaphore_signal(barrier, inc=1, device_id={"pipe": other})
    for step in range(1, replicas):
        peer = lax.rem(me + step, replicas)
        pl.semaphore_signal(barrier, inc=1, device_id={"dp": peer})
    pl.semaphore_wait(barrier, 2 + replicas - 1)
    load_w.wait()

    def act_copy(m, cols=None):
        where = (rows_of(m),) if cols is None else (rows_of(m), cols)
        return pltpu.make_async_remote_copy(
            src_ref=acts.at[where], dst_ref=xs.at[where],
            send_sem=act_send.at[m], recv_sem=act_recv.at[m], device_id={"pipe": after},
        )

    def down_copy(m, cols=None):
        where = (rows_of(m),) if cols is None else (rows_of(m), cols)
        return pltpu.make_async_remote_copy(
            src_ref=acts.at[where], dst_ref=ups.at[where],
            send_sem=down_send.at[m], recv_sem=down_recv.at[m], device_id={"pipe": before},
        )

    def norm_copy(m, step):
        peer = lax.rem(me + step, replicas)
        cols = pl.ds(pl.multiple_of(peer * chunk, chunk), chunk)
        return pltpu.make_async_remote_copy(
            src_ref=normed.at[rows_of(m), cols], dst_ref=normed_in.at[me, rows_of(m)],
            send_sem=norm_send.at[step, m], recv_sem=norm_recv.at[step, m],
            device_id={"dp": peer},
        )

    def norm_arrival(m, step):
        origin = lax.rem(me + replicas - step, replicas)
        return pltpu.make_async_remote_copy(
            src_ref=normed.at[rows_of(m), pl.ds(0, chunk)],
            dst_ref=normed_in.at[origin, rows_of(m)],
            send_sem=norm_send.at[step, m], recv_sem=norm_recv.at[step, m],
            device_id={"dp": origin},
        )

    def slope_copy(origin, m, to, sends):
        block = slopes.at[origin, rows_of(m)]
        return pltpu.make_async_remote_copy(
            src_ref=block, dst_ref=block,
            send_sem=sends.at[origin, m], recv_sem=slope_recv.at[origin, m],
            device_id={"dp": to},
        )

    def go_right(origin, m):
        return slope_copy(origin, m, me + 1, right_send)

    def go_left(origin, m):
        return slope_copy(origin, m, me - 1, left_send)

    def forward(m):
        here = rows_of(m)

        @pl.when(is_first)
        def _():
            load_first(m).wait()

        @pl.when(jnp.logical_not(is_first))
        def _():
            act_copy(m).wait_recv()

        def squares(n, total):
            part = xs[here, cols_of(n)].astype(jnp.float32)
            return total + jnp.sum(part * part, axis=-1, keepdims=True)

        total = lax.fori_loop(0, tiles, squares, jnp.zeros((rows, 1), jnp.float32))
        fac = lax.rsqrt(total / width + EPSILON)
        facs[here, :] = jnp.broadcast_to(fac, (rows, 128))

        @pl.loop(0, tiles)
        def _(n):
            part = xs[here, cols_of(n)].astype(jnp.float32)
            normed[here, cols_of(n)] = (part * fac).astype(jnp.bfloat16)

        for step in range(1, replicas):
            norm_copy(m, step).start()

        @pl.loop(0, tiles)
        def _(n):
            cols = cols_of(n)
            gate = jnp.dot(normed[here, :], w[:, cols], preferred_element_type=jnp.float32)
            gates[here, cols] = gate
            out = xs[here, cols].astype(jnp.float32) + gate / (1.0 + jnp.exp(-gate))
            acts[here, cols] = out.astype(jnp.bfloat16)

            @pl.when(jnp.logical_not(is_last))
            def _():
                act_copy(m, cols).start()

    def backward(m):
        here = rows_of(m)

        @pl.when(is_last)
        def _():
            load_cot(m).wait()

        @pl.when(jnp.logical_not(is_last))
        def _():
            act_copy(m).wait_send()
            down_copy(m).wait_recv()

        @pl.loop(0, tiles)
        def _(n):
            cols = cols_of(n)
            gate = gates[here, cols]
            sig = 1.0 / (1.0 + jnp.exp(-gate))
            up = ups[here, cols].astype(jnp.float32)
            slope = up * sig * (1.0 + gate * (1.0 - sig))
            slopes[me, here, cols] = slope.astype(jnp.bfloat16)

        @pl.when(me < replicas - 1)
        def _():
            go_right(me, m).start()

        @pl.when(me > 0)
        def _():
            go_left(me, m).start()

        fac = facs[here, pl.ds(0, 1)]

        @pl.when(jnp.logical_not(is_first))
        def _():
            def back_tile(n, total):
                cols = cols_of(n)
                back = lax.dot_general(
                    slopes[me, here, :], w[cols, :], (((1,), (1,)), ((), ())),
                    preferred_element_type=jnp.float32,
                )
                gates[here, cols] = back
                unit = xs[here, cols].astype(jnp.float32) * fac
                return total + jnp.sum(back * unit, axis=-1, keepdims=True)

            total = lax.fori_loop(0, tiles, back_tile, jnp.zeros((rows, 1), jnp.float32))
            mean = total / width

            @pl.loop(0, tiles)
            def _(n):
                cols = cols_of(n)
                unit = xs[here, cols].astype(jnp.float32) * fac
                down = ups[here, cols].astype(jnp.float32) + fac * (gates[here, cols] - unit * mean)
                acts[here, cols] = down.astype(jnp.bfloat16)
                down_copy(m, cols).start()

    lag = jnp.minimum(sections - 1 - section, micro - 1)

    @pl.loop(0, 2 * micro - 1)
    def _(t):
        @pl.when(t < micro)
        def _():
            forward(t)

        @pl.when(jnp.logical_and(t >= lag, t < lag + micro))
        def _():
            backward(t - lag)

    for step in range(1, replicas):
        @pl.loop(0, micro)
        def _(m):
            norm_arrival(m, step).wait_recv()

    own = pl.ds(pl.multiple_of(me * chunk, chunk), chunk)
    normed_in[me] = normed[:, own]
    for origin in range(replicas):
        normed_t[:, pl.ds(origin * tokens, tokens)] = normed_in[origin].T

    def add_origin(origin, start):
        left = pl.ds(pl.multiple_of(origin * tokens, tokens), tokens)

        @pl.loop(0, width // OUT_TILE)
        def _(n):
            cols = pl.ds(pl.multiple_of(n * OUT_TILE, OUT_TILE), OUT_TILE)
            term = jnp.dot(
                normed_t[:, left], slopes[origin, :, cols], preferred_element_type=jnp.float32
            )
            sums[:, cols] = term if start else sums[:, cols] + term

    add_origin(me, True)

    for far in range(1, replicas):
        @pl.loop(0, micro)
        def _(m):
            @pl.when(me - far >= 0)
            def _():
                go_right(me - far, m).wait_recv()

                @pl.when(me < replicas - 1)
                def _():
                    go_right(me - far, m).start()

            @pl.when(me + far < replicas)
            def _():
                go_left(me + far, m).wait_recv()

                @pl.when(me > 0)
                def _():
                    go_left(me + far, m).start()

        @pl.when(me - far >= 0)
        def _():
            add_origin(me - far, False)

        @pl.when(me + far < replicas)
        def _():
            add_origin(me + far, False)

    scale = 1.0 / math.sqrt(tokens * replicas)

    @pl.loop(0, width // OUT_TILE)
    def _(n):
        cols = pl.ds(pl.multiple_of(n * OUT_TILE, OUT_TILE), OUT_TILE)
        out_ref[:, cols] = (sums[:, cols] * scale).astype(jnp.bfloat16)

    @pl.loop(0, micro)
    def _(m):
        for step in range(1, replicas):
            norm_copy(m, step).wait_send()

        @pl.when(jnp.logical_not(is_first))
        def _():
            down_copy(m).wait_send()

        for origin in range(replicas):
            @pl.when(jnp.logical_and(me >= origin, me < replicas - 1))
            def _():
                go_right(origin, m).wait_send()

            @pl.when(jnp.logical_and(me <= origin, me > 0))
            def _():
                go_left(origin, m).wait_send()


def on_device(sections, replicas, inputs, projection, cotangent):
    micro, rows, width = inputs.shape
    tokens = micro * rows
    chunk = width // replicas
    bf16, f32 = jnp.bfloat16, jnp.float32
    dma = pltpu.SemaphoreType.DMA
    out = pl.pallas_call(
        functools.partial(relay_kernel, micro, sections, replicas),
        out_shape=jax.ShapeDtypeStruct((chunk, width), bf16),
        in_specs=[pl.BlockSpec(memory_space=pl.ANY)] * 3,
        out_specs=pl.BlockSpec(memory_space=pltpu.VMEM),
        scratch_shapes=[
            pltpu.VMEM((width, width), bf16),
            pltpu.VMEM((tokens, width), bf16),
            pltpu.VMEM((tokens, width), bf16),
            pltpu.VMEM((tokens, width), f32),
            pltpu.VMEM((tokens, width), bf16),
            pltpu.VMEM((replicas, tokens, width), bf16),
            pltpu.VMEM((tokens, width), bf16),
            pltpu.VMEM((replicas, tokens, chunk), bf16),
            pltpu.VMEM((chunk, replicas * tokens), bf16),
            pltpu.VMEM((tokens, 128), f32),
            pltpu.VMEM((chunk, width), f32),
            dma, dma((micro,)), dma((micro,)),
            dma((micro,)), dma((micro,)), dma((micro,)), dma((micro,)),
            dma((replicas, micro)), dma((replicas, micro)),
            dma((replicas, micro)), dma((replicas, micro)), dma((replicas, micro)),
        ],
        compiler_params=pltpu.CompilerParams(
            collective_id=0, has_side_effects=True, vmem_limit_bytes=64 * 1024 * 1024
        ),
        cost_estimate=pl.CostEstimate(
            flops=6 * tokens * width * width,
            bytes_accessed=2 * width * (width + 2 * tokens + chunk),
            transcendentals=2 * tokens * width,
        ),
    )(inputs.reshape(tokens, width), projection[0], cotangent.reshape(tokens, width))
    return out[None]


def solution(mesh):
    placed = (P(None, "dp", None), P("pipe", None, None), P(None, "dp", None))
    body = functools.partial(on_device, mesh.shape["pipe"], mesh.shape["dp"])
    return jax.shard_map(
        body, mesh=mesh, in_specs=placed, out_specs=P("pipe", "dp", None), check_vma=False
    )
```

```python
import functools
import math

import jax
import jax.numpy as jnp
from jax import lax
from jax.experimental import pallas as pl
from jax.experimental.pallas import tpu as pltpu
from jax.sharding import PartitionSpec as P

EPSILON = 1e-06
TILE = 512
OUT_TILE = 256


def relay_kernel(
    micro, sections, replicas,
    in_ref, w_hbm, cot_ref, out_ref,
    w, xs, acts, gates, ups, slopes, normed, normed_in, normed_t, facs, sums,
    w_sem, first_sem, cot_sem, act_send, act_recv, down_send, down_recv,
    norm_send, norm_recv, right_send, left_send, slope_recv,
):
    section = lax.axis_index("pipe")
    me = lax.axis_index("dp")
    tokens, width = xs.shape
    rows = tokens // micro
    chunk = width // replicas
    tiles = width // TILE
    is_first = section == 0
    is_last = section == sections - 1
    after = lax.rem(section + 1, sections)
    before = lax.rem(section + sections - 1, sections)

    def rows_of(m):
        return pl.ds(pl.multiple_of(m * rows, rows), rows)

    def cols_of(n):
        return pl.ds(pl.multiple_of(n * TILE, TILE), TILE)

    load_w = pltpu.make_async_copy(w_hbm, w, w_sem)
    load_w.start()

    def load_first(m):
        return pltpu.make_async_copy(in_ref.at[rows_of(m)], xs.at[rows_of(m)], first_sem.at[m])

    def load_cot(m):
        return pltpu.make_async_copy(cot_ref.at[rows_of(m)], ups.at[rows_of(m)], cot_sem.at[m])

    @pl.when(is_first)
    def _():
        @pl.loop(0, micro)
        def _(m):
            load_first(m).start()

    @pl.when(is_last)
    def _():
        @pl.loop(0, micro)
        def _(m):
            load_cot(m).start()

    barrier = pltpu.get_barrier_semaphore()
    for other in (after, before):
        pl.semaphore_signal(barrier, inc=1, device_id={"pipe": other})
    for step in range(1, replicas):
        peer = lax.rem(me + step, replicas)
        pl.semaphore_signal(barrier, inc=1, device_id={"dp": peer})
    pl.semaphore_wait(barrier, 2 + replicas - 1)
    load_w.wait()

    def act_copy(m, cols=None):
        where = (rows_of(m),) if cols is None else (rows_of(m), cols)
        return pltpu.make_async_remote_copy(
            src_ref=acts.at[where], dst_ref=xs.at[where],
            send_sem=act_send.at[m], recv_sem=act_recv.at[m], device_id={"pipe": after},
        )

    def down_copy(m, cols=None):
        where = (rows_of(m),) if cols is None else (rows_of(m), cols)
        return pltpu.make_async_remote_copy(
            src_ref=acts.at[where], dst_ref=ups.at[where],
            send_sem=down_send.at[m], recv_sem=down_recv.at[m], device_id={"pipe": before},
        )

    def norm_copy(m, step):
        peer = lax.rem(me + step, replicas)
        cols = pl.ds(pl.multiple_of(peer * chunk, chunk), chunk)
        return pltpu.make_async_remote_copy(
            src_ref=normed.at[rows_of(m), cols], dst_ref=normed_in.at[me, rows_of(m)],
            send_sem=norm_send.at[step, m], recv_sem=norm_recv.at[step, m],
            device_id={"dp": peer},
        )

    def norm_arrival(m, step):
        origin = lax.rem(me + replicas - step, replicas)
        return pltpu.make_async_remote_copy(
            src_ref=normed.at[rows_of(m), pl.ds(0, chunk)],
            dst_ref=normed_in.at[origin, rows_of(m)],
            send_sem=norm_send.at[step, m], recv_sem=norm_recv.at[step, m],
            device_id={"dp": origin},
        )

    def slope_copy(origin, m, to, sends):
        block = slopes.at[origin, rows_of(m)]
        return pltpu.make_async_remote_copy(
            src_ref=block, dst_ref=block,
            send_sem=sends.at[origin, m], recv_sem=slope_recv.at[origin, m],
            device_id={"dp": to},
        )

    def go_right(origin, m):
        return slope_copy(origin, m, me + 1, right_send)

    def go_left(origin, m):
        return slope_copy(origin, m, me - 1, left_send)

    def forward(m):
        here = rows_of(m)

        @pl.when(is_first)
        def _():
            load_first(m).wait()

        @pl.when(jnp.logical_not(is_first))
        def _():
            act_copy(m).wait_recv()

        def squares(n, total):
            part = xs[here, cols_of(n)].astype(jnp.float32)
            return total + jnp.sum(part * part, axis=-1, keepdims=True)

        total = lax.fori_loop(0, tiles, squares, jnp.zeros((rows, 1), jnp.float32))
        fac = lax.rsqrt(total / width + EPSILON)
        facs[here, :] = jnp.broadcast_to(fac, (rows, 128))

        @pl.loop(0, tiles)
        def _(n):
            cols = cols_of(n)
            gate = fac * jnp.dot(xs[here, :], w[:, cols], preferred_element_type=jnp.float32)
            gates[here, cols] = gate
            out = xs[here, cols].astype(jnp.float32) + gate / (1.0 + jnp.exp(-gate))
            acts[here, cols] = out.astype(jnp.bfloat16)

            @pl.when(jnp.logical_not(is_last))
            def _():
                act_copy(m, cols).start()

        @pl.loop(0, tiles)
        def _(n):
            part = xs[here, cols_of(n)].astype(jnp.float32)
            normed[here, cols_of(n)] = (part * fac).astype(jnp.bfloat16)

        for step in range(1, replicas):
            norm_copy(m, step).start()

    def backward(m):
        here = rows_of(m)

        @pl.when(is_last)
        def _():
            load_cot(m).wait()

        @pl.when(jnp.logical_not(is_last))
        def _():
            act_copy(m).wait_send()
            down_copy(m).wait_recv()

        def slope_tile(n, total):
            cols = cols_of(n)
            gate = gates[here, cols]
            sig = 1.0 / (1.0 + jnp.exp(-gate))
            up = ups[here, cols].astype(jnp.float32)
            slope = (up * sig * (1.0 + gate * (1.0 - sig))).astype(jnp.bfloat16)
            slopes[me, here, cols] = slope
            return total + jnp.sum(slope.astype(jnp.float32) * gate, axis=-1, keepdims=True)

        total = lax.fori_loop(0, tiles, slope_tile, jnp.zeros((rows, 1), jnp.float32))
        mean = total / width

        @pl.when(me < replicas - 1)
        def _():
            go_right(me, m).start()

        @pl.when(me > 0)
        def _():
            go_left(me, m).start()

        fac = facs[here, pl.ds(0, 1)]

        @pl.when(jnp.logical_not(is_first))
        def _():
            @pl.loop(0, tiles)
            def _(n):
                cols = cols_of(n)
                back = lax.dot_general(
                    slopes[me, here, :], w[cols, :], (((1,), (1,)), ((), ())),
                    preferred_element_type=jnp.float32,
                )
                unit = xs[here, cols].astype(jnp.float32) * fac
                down = ups[here, cols].astype(jnp.float32) + fac * (back - unit * mean)
                acts[here, cols] = down.astype(jnp.bfloat16)
                down_copy(m, cols).start()

    lag = jnp.minimum(sections - 1 - section, micro - 1)

    @pl.loop(0, 2 * micro - 1)
    def _(t):
        @pl.when(t < micro)
        def _():
            forward(t)

        @pl.when(jnp.logical_and(t >= lag, t < lag + micro))
        def _():
            backward(t - lag)

    for step in range(1, replicas):
        @pl.loop(0, micro)
        def _(m):
            norm_arrival(m, step).wait_recv()

    own = pl.ds(pl.multiple_of(me * chunk, chunk), chunk)
    normed_in[me] = normed[:, own]
    for origin in range(replicas):
        normed_t[:, pl.ds(origin * tokens, tokens)] = normed_in[origin].T

    def add_origin(origin, start):
        left = pl.ds(pl.multiple_of(origin * tokens, tokens), tokens)

        @pl.loop(0, width // OUT_TILE)
        def _(n):
            cols = pl.ds(pl.multiple_of(n * OUT_TILE, OUT_TILE), OUT_TILE)
            term = jnp.dot(
                normed_t[:, left], slopes[origin, :, cols], preferred_element_type=jnp.float32
            )
            sums[:, cols] = term if start else sums[:, cols] + term

    add_origin(me, True)

    for far in range(1, replicas):
        @pl.loop(0, micro)
        def _(m):
            @pl.when(me - far >= 0)
            def _():
                go_right(me - far, m).wait_recv()

                @pl.when(me < replicas - 1)
                def _():
                    go_right(me - far, m).start()

            @pl.when(me + far < replicas)
            def _():
                go_left(me + far, m).wait_recv()

                @pl.when(me > 0)
                def _():
                    go_left(me + far, m).start()

        @pl.when(me - far >= 0)
        def _():
            add_origin(me - far, False)

        @pl.when(me + far < replicas)
        def _():
            add_origin(me + far, False)

    scale = 1.0 / math.sqrt(tokens * replicas)

    @pl.loop(0, width // OUT_TILE)
    def _(n):
        cols = pl.ds(pl.multiple_of(n * OUT_TILE, OUT_TILE), OUT_TILE)
        out_ref[:, cols] = (sums[:, cols] * scale).astype(jnp.bfloat16)

    @pl.loop(0, micro)
    def _(m):
        for step in range(1, replicas):
            norm_copy(m, step).wait_send()

        @pl.when(jnp.logical_not(is_first))
        def _():
            down_copy(m).wait_send()

        for origin in range(replicas):
            @pl.when(jnp.logical_and(me >= origin, me < replicas - 1))
            def _():
                go_right(origin, m).wait_send()

            @pl.when(jnp.logical_and(me <= origin, me > 0))
            def _():
                go_left(origin, m).wait_send()


def on_device(sections, replicas, inputs, projection, cotangent):
    micro, rows, width = inputs.shape
    tokens = micro * rows
    chunk = width // replicas
    bf16, f32 = jnp.bfloat16, jnp.float32
    dma = pltpu.SemaphoreType.DMA
    out = pl.pallas_call(
        functools.partial(relay_kernel, micro, sections, replicas),
        out_shape=jax.ShapeDtypeStruct((chunk, width), bf16),
        in_specs=[pl.BlockSpec(memory_space=pl.ANY)] * 3,
        out_specs=pl.BlockSpec(memory_space=pltpu.VMEM),
        scratch_shapes=[
            pltpu.VMEM((width, width), bf16),
            pltpu.VMEM((tokens, width), bf16),
            pltpu.VMEM((tokens, width), bf16),
            pltpu.VMEM((tokens, width), f32),
            pltpu.VMEM((tokens, width), bf16),
            pltpu.VMEM((replicas, tokens, width), bf16),
            pltpu.VMEM((tokens, width), bf16),
            pltpu.VMEM((replicas, tokens, chunk), bf16),
            pltpu.VMEM((chunk, replicas * tokens), bf16),
            pltpu.VMEM((tokens, 128), f32),
            pltpu.VMEM((chunk, width), f32),
            dma, dma((micro,)), dma((micro,)),
            dma((micro,)), dma((micro,)), dma((micro,)), dma((micro,)),
            dma((replicas, micro)), dma((replicas, micro)),
            dma((replicas, micro)), dma((replicas, micro)), dma((replicas, micro)),
        ],
        compiler_params=pltpu.CompilerParams(
            collective_id=0, has_side_effects=True, vmem_limit_bytes=64 * 1024 * 1024
        ),
        cost_estimate=pl.CostEstimate(
            flops=6 * tokens * width * width,
            bytes_accessed=2 * width * (width + 2 * tokens + chunk),
            transcendentals=2 * tokens * width,
        ),
    )(inputs.reshape(tokens, width), projection[0], cotangent.reshape(tokens, width))
    return out[None]


def solution(mesh):
    placed = (P(None, "dp", None), P("pipe", None, None), P(None, "dp", None))
    body = functools.partial(on_device, mesh.shape["pipe"], mesh.shape["dp"])
    return jax.shard_map(
        body, mesh=mesh, in_specs=placed, out_specs=P("pipe", "dp", None), check_vma=False
    )
```
